256 devices in a mesh: freq: 2 (over y_lo), row: 32 (over x, z), col: 4 (over y_hi, core).
Axes of the slice: x: 4, y: 4 (y_hi: 2, y_lo: 2; y = y_hi * 2 + y_lo), z: 8, core: 2. Of those that a mesh axis runs over, the one named last changes fastest.
Arguments:
- reflection: bfloat16 [8, 2, 8192, 8192], P('freq', None, 'row', 'col'), may hold values from -0.046875 to 0.046875
- panels: bfloat16 [8, 2, 2, 16, 8192], P('freq', None, None, None, ('col', 'row')), may hold values from -6 to 6
- onsets: int32 [16, 8192], P(None, 'row'), may hold values from 128 to 1024
Outputs:
- updates: float32 [32, 1024, 8192], P('col', 'freq', 'row')
The draws below stay inside these ranges and needn't reach their ends.
All inputs are finite; a program needn't handle non-finite values.
Results may differ from the reference program's by a relative error of at most 0.0003.
Values may be sent and summed in bfloat16 or wider, within the bound.
A program may use at most 64 MiB of HBM per device.

```python
import jax
import jax.numpy as jnp
from jax import lax

NR = 8192
NS = 8192
NFOC = 16
NT = 1024
NFREQ = 8


def set_ends(drawn, stream_key, least, largest):
    shape = drawn.shape
    spot = [jax.random.randint(jax.random.fold_in(stream_key, axis), (), 0, shape[axis]) for axis in range(len(shape))]
    drawn = drawn.at[tuple(spot)].set(least)
    longest = shape.index(max(shape))
    spot[longest] = (spot[longest] + 1) % shape[longest]
    return drawn.at[tuple(spot)].set(largest)


def level_of(own_key, shape, cuts, least, largest):
    def one(position, parts):
        heights = jax.random.uniform(jax.random.fold_in(jax.random.fold_in(own_key, 6), position), (parts,), jnp.float32, least / len(cuts), largest / len(cuts))
        return jnp.repeat(jnp.exp(heights), shape[position] // parts).reshape((-1,) + (1,) * (len(shape) - position - 1))

    level = one(*cuts[0])
    for cut in cuts[1:]:
        level = level * one(*cut)
    return level


def normal_values(key, shape, scale, most, split=(), held_as=jnp.bfloat16):
    level = level_of(key, shape, split, -0.22, 0.18) if split else 1.0
    entries = jax.random.normal(key, shape, jnp.float32) * scale * level
    return jnp.minimum(jnp.maximum(entries, -most), most).astype(held_as)


def setup_inputs(seed: int = 0) -> dict:
    streams_of = jax.random.split(jax.random.key(seed), 4)
    reflection = normal_values(streams_of[0], (NFREQ, 2, NR, NS), (2 * NS) ** -0.5, 0.046875, ((0, 2), (2, 32), (3, 4)))
    panels = normal_values(streams_of[1], (NFREQ, 2, 2, NFOC, NS), 1.0, 6.0, ((0, 2), (4, 128)))
    onsets = set_ends(jax.random.randint(streams_of[2], (NFOC, NR), NT // 8, NT + 1), jax.random.fold_in(streams_of[2], 1), NT // 8, NT).astype(jnp.int32)
    return dict(reflection=reflection, panels=panels, onsets=onsets)


decay = 2.0
bin_step = 37

def products(reflection_k, panel_k):
    dims = (((1,), (1,)), ((), ()))
    real_rows = jnp.concatenate([panel_k[0, 0], panel_k[0, 1]], axis=0)
    imag_rows = jnp.concatenate([panel_k[1, 0], panel_k[1, 1]], axis=0)
    first = lax.dot_general(real_rows, reflection_k[0], dims, preferred_element_type=jnp.float32)
    second = lax.dot_general(imag_rows, reflection_k[1], dims, preferred_element_type=jnp.float32)
    third = lax.dot_general(imag_rows, reflection_k[0], dims, preferred_element_type=jnp.float32)
    fourth = lax.dot_general(real_rows, reflection_k[1], dims, preferred_element_type=jnp.float32)
    count = panel_k.shape[2]
    signs = jnp.concatenate([jnp.ones((count,), jnp.float32), -jnp.ones((count,), jnp.float32)])[:, None]
    return jnp.stack([first - signs * second, third + signs * fourth], axis=0)

def reference(reflection, panels, onsets):
    spectra = lax.map(lambda pair: products(pair[0], pair[1]), (reflection, panels))
    times = jnp.arange(NT, dtype=jnp.int32)
    bins = bin_step * (jnp.arange(NFREQ, dtype=jnp.int32) + 1)
    phase_int = bins[:, None] * times[None, :] % NT
    phase = phase_int.astype(jnp.float32) * jnp.float32(2.0 * 3.141592653589793 / NT)
    cosine = jnp.cos(phase)
    sine = jnp.sin(phase)
    series = jnp.einsum('kcr,kt->ctr', spectra[:, 0], cosine, precision=lax.Precision.HIGHEST)
    series = series - jnp.einsum('kcr,kt->ctr', spectra[:, 1], sine, precision=lax.Precision.HIGHEST)
    weight = jnp.exp(-decay * times.astype(jnp.float32) / NT) / jnp.sqrt(jnp.float32(NFREQ))
    stacked = jnp.concatenate([onsets, onsets], axis=0)
    keep = times[None, :, None] < stacked[:, None, :]
    return jnp.where(keep, series * weight[None, :, None], jnp.float32(0.0))
```

```python
import functools

import jax
import jax.numpy as jnp
import ml_dtypes
import numpy as np
from jax import lax
from jax.experimental import pallas as pl
from jax.experimental.pallas import tpu as pltpu
from jax.sharding import PartitionSpec as P

NT = 1024
decay = 2.0
bin_step = 37

MESH = pl.DeviceIdType.MESH
BF16 = jnp.bfloat16
F32 = jnp.float32

NX, NZ = 4, 8
FREQS = 4
CHUNKS = 2
PER = FREQS // CHUNKS
NFOC = 16
OWN = 3

GROUPS = ((3, 1), (1, 2), (4, 2), (0, 1), (6, 2))
XSTEPS = (1, 3, 2)


def gather_kernel(
    refl, panels, out, rbuf, praw, held, pmat, sendbuf, slots, load_sem, z_send, z_recv, x_send, x_recv, e_send, e_recv
):
    freq = lax.axis_index("freq")
    row = lax.axis_index("row")
    col = lax.axis_index("col")
    x, z = row // NZ, row % NZ

    def along_z(d):
        return {"row": x * NZ + (z + d + NZ) % NZ}

    def along_x(d):
        return {"row": ((x + d) % NX) * NZ + z}

    def peer(a, b):
        c = (col // 2 + b // 2) % 2 * 2 + (col + b) % 2
        return {"freq": (freq + a) % 2, "col": c}

    peers = [(a, b) for a in range(2) for b in range(4) if (a, b) != (0, 0)]

    barrier = pltpu.get_barrier_semaphore()
    near = [along_z(d) for d in (1, -1, 2, -2)] + [along_x(d) for d in XSTEPS]
    near += [peer(a, b) for a, b in peers]
    for device in near:
        pl.semaphore_signal(barrier, inc=1, device_id=device, device_id_type=MESH)

    load_panels = pltpu.make_async_copy(panels, praw, load_sem.at[FREQS])
    load_panels.start()
    loads = [pltpu.make_async_copy(refl.at[f], rbuf.at[f], load_sem.at[f]) for f in range(FREQS)]
    for load in loads:
        load.start()
    load_panels.wait()

    odd = (z % 2) == 1
    for f in range(FREQS):
        for d in range(2):
            re = praw[f, 0, d].astype(F32)
            im = praw[f, 1, d].astype(F32)
            left = jnp.where(odd, im, re)
            right = jnp.where(odd, re, im)
            held[f // PER, 0, OWN, d, f % PER] = jnp.concatenate([left, right], axis=1).astype(BF16)

    pl.semaphore_wait(barrier, len(near))

    started = []

    def z_copy(c, i, src, dst, step):
        return pltpu.make_async_remote_copy(
            src_ref=held.at[(c, 0) + src],
            dst_ref=held.at[(c, 0) + dst],
            send_sem=z_send.at[c, i],
            recv_sem=z_recv.at[c, i],
            device_id=along_z(step),
            device_id_type=MESH,
        )

    first = ((1, 0), (-1, 1), (2, 2), (-2, 3))

    def z_first(c, step, i):
        return z_copy(c, i, (OWN,), (OWN - step,), step)

    def z_second(c):
        return [
            z_copy(c, 4, (OWN - 2,), (OWN - 3,), 1),
            z_copy(c, 5, (OWN + 2,), (OWN + 3,), -1),
            z_copy(c, 6, (OWN - 2, 0), (OWN + 4, 0), 2),
            z_copy(c, 7, (OWN + 2, 1), (OWN + 4, 1), -2),
        ]

    def x_copies(c, g):
        at, count = GROUPS[g]
        return [
            pltpu.make_async_remote_copy(
                src_ref=held.at[c, 0, pl.ds(at, count)],
                dst_ref=held.at[c, (NX - step) % NX, pl.ds(at, count)],
                send_sem=x_send.at[c, g, i],
                recv_sem=x_recv.at[c, g, i],
                device_id=along_x(step),
                device_id_type=MESH,
            )
            for i, step in enumerate(XSTEPS)
        ]

    def start(copies):
        for copy in copies:
            copy.start()
            started.append(copy)

    for c in range(CHUNKS):
        start([z_first(c, step, i) for step, i in first])
        start(x_copies(c, 0))
    for c in range(CHUNKS):
        for step, i in first:
            z_first(c, step, i).wait_recv()
        start(z_second(c))
        start(x_copies(c, 1))
        start(x_copies(c, 2))
    for c in range(CHUNKS):
        for copy in z_second(c):
            copy.wait_recv()
        start(x_copies(c, 3))
        start(x_copies(c, 4))

    def e_copy(f, a, b):
        c = (col // 2 + b // 2) % 2 * 2 + (col + b) % 2
        return pltpu.make_async_remote_copy(
            src_ref=sendbuf.at[f, c],
            dst_ref=slots.at[a, f, b],
            send_sem=e_send.at[f, a, b],
            recv_sem=e_recv.at[f, a, b],
            device_id=peer(a, b),
            device_id_type=MESH,
        )

    over_sources = (((1,), (1,)), ((), ()))
    lower = lax.broadcasted_iota(jnp.int32, (NFOC, 128), 1) < 64
    for c in range(CHUNKS):
        for g in range(len(GROUPS)):
            for copy in x_copies(c, g):
                copy.wait_recv()
        for i in range(PER):
            f = c * PER + i
            for d in range(2):
                for xa in range(NX):
                    xs = (xa - x + NX) % NX
                    for zp in range(NZ // 2):
                        even = held[c, xs, (2 * zp - z + OWN + NZ) % NZ, d, i].astype(F32)
                        uneven = held[c, xs, (2 * zp + 1 - z + OWN + NZ) % NZ, d, i].astype(F32)
                        at = (xa * NZ // 2 + zp) * 128
                        re = jnp.where(lower, even, uneven)
                        im = pltpu.roll(jnp.where(lower, uneven, even), 64, 1)
                        pmat[pl.ds(d * 16, 16), pl.ds(at, 128)] = re.astype(BF16)
                        pmat[pl.ds(32 + d * 16, 16), pl.ds(at, 128)] = im.astype(BF16)
            loads[f].wait()
            with_re = lax.dot_general(pmat[...], rbuf[f, 0], over_sources, preferred_element_type=F32)
            with_im = lax.dot_general(pmat[...], rbuf[f, 1], over_sources, preferred_element_type=F32)
            for q in range(4):
                here = slice(8 * q, 8 * q + 8)
                there = slice(32 + 8 * q, 40 + 8 * q)
                if q < 2:
                    sendbuf[f, q, 0] = with_re[here] - with_im[there]
                    sendbuf[f, q, 1] = with_re[there] + with_im[here]
                else:
                    sendbuf[f, q, 0] = with_re[here] + with_im[there]
                    sendbuf[f, q, 1] = with_re[there] - with_im[here]
            start([e_copy(f, a, b) for a, b in peers])

    def keep(k, part, value):
        for h in range(out.shape[0]):
            out[h, pl.ds((k * 2 + part) * 8, 8), :] = value[:, 128 * h : 128 * h + 128]

    for f in range(FREQS):
        for a, b in peers:
            e_copy(f, a, b).wait_recv()
        for part in range(2):
            near_sum = sendbuf[f, col, part] + slots[0, f, 1, part]
            near_sum += slots[0, f, 2, part] + slots[0, f, 3, part]
            keep(f, part, near_sum)
            far_sum = slots[1, f, 0, part] + slots[1, f, 1, part]
            far_sum += slots[1, f, 2, part] + slots[1, f, 3, part]
            keep(f + FREQS, part, far_sum)
    for copy in started:
        copy.wait_send()


def times_kernel(spectra, table, onsets, out, series, out_sem):
    freq = lax.axis_index("freq")
    col = lax.axis_index("col")
    steps = series.shape[1]
    width = series.shape[2]
    basis = table[freq]
    times = freq * steps + lax.broadcasted_iota(jnp.int32, (steps, width), 0)
    limits = onsets[pl.ds(pl.multiple_of(col % 2 * 8, 8), 8), :]
    copies = []
    for c in range(8):
        values = jnp.concatenate(
            [spectra[h, pl.ds(c, 16, stride=8), :] for h in range(width // 128)], axis=1
        )
        high = values.astype(BF16)
        low = (values - high.astype(F32)).astype(BF16)
        parts = jnp.concatenate([high, high, low, low], axis=0)
        found = jnp.dot(basis, parts, preferred_element_type=F32)
        series[c] = jnp.where(times < limits[c : c + 1, :], found, 0.0)
        copy = pltpu.make_async_copy(series.at[c], out.at[c], out_sem.at[c])
        copy.start()
        copies.append(copy)
    for copy in copies:
        copy.wait()


def make_table(groups, freq_here):
    total = groups * freq_here
    t = np.arange(NT, dtype=np.int64)
    weight = np.exp(-decay * t / NT) / np.sqrt(total)
    halves = []
    for g in range(groups):
        mine = slice(g * NT // groups, (g + 1) * NT // groups)
        columns = []
        for a in range(groups):
            for f in range(freq_here):
                k = (g + a) % groups * freq_here + f
                phase = 2.0 * np.pi * ((bin_step * (k + 1) * t) % NT) / NT
                columns += [(np.cos(phase) * weight)[mine], (-np.sin(phase) * weight)[mine]]
        whole = np.stack(columns, axis=1)
        high = whole.astype(np.float32).astype(ml_dtypes.bfloat16)
        low = (whole - high.astype(np.float64)).astype(np.float32).astype(ml_dtypes.bfloat16)
        halves.append(np.concatenate([high, low, high, low], axis=1))
    return np.stack(halves)


def shards(reflection, panels, onsets):
    receivers = reflection.shape[2]
    sources = reflection.shape[3]
    vmem = pl.BlockSpec(memory_space=pltpu.VMEM)
    hbm = pl.BlockSpec(memory_space=pl.ANY)
    spectra = pl.pallas_call(
        gather_kernel,
        out_shape=jax.ShapeDtypeStruct((receivers // 128, 128, 128), F32),
        in_specs=[hbm, hbm],
        out_specs=vmem,
        scratch_shapes=[
            pltpu.VMEM(reflection.shape, BF16),
            pltpu.VMEM(panels.shape, BF16),
            pltpu.VMEM((CHUNKS, NX, NZ, 2, PER, NFOC, 128), BF16),
            pltpu.VMEM((64, sources), BF16),
            pltpu.VMEM((FREQS, 4, 2, 8, receivers), F32),
            pltpu.VMEM((2, FREQS, 4, 2, 8, receivers), F32),
            pltpu.SemaphoreType.DMA((FREQS + 1,)),
            pltpu.SemaphoreType.DMA((CHUNKS, 8)),
            pltpu.SemaphoreType.DMA((CHUNKS, 8)),
            pltpu.SemaphoreType.DMA((CHUNKS, len(GROUPS), 3)),
            pltpu.SemaphoreType.DMA((CHUNKS, len(GROUPS), 3)),
            pltpu.SemaphoreType.DMA((FREQS, 2, 4)),
            pltpu.SemaphoreType.DMA((FREQS, 2, 4)),
        ],
        compiler_params=pltpu.CompilerParams(collective_id=0, has_side_effects=True, vmem_limit_bytes=48 << 20),
        name="gather_products",
    )(reflection, panels)
    groups = lax.axis_size("freq")
    steps = NT // groups
    table = jnp.asarray(make_table(groups, reflection.shape[0]))
    return pl.pallas_call(
        times_kernel,
        out_shape=jax.ShapeDtypeStruct((8, steps, receivers), F32),
        in_specs=[vmem, vmem, vmem],
        out_specs=hbm,
        scratch_shapes=[pltpu.VMEM((8, steps, receivers), F32), pltpu.SemaphoreType.DMA((8,))],
        compiler_params=pltpu.CompilerParams(vmem_limit_bytes=48 << 20),
        name="to_times",
    )(spectra, table, onsets)


def solution(mesh):
    return jax.shard_map(
        shards,
        mesh=mesh,
        in_specs=(
            P("freq", None, "row", "col"),
            P("freq", None, None, None, ("col", "row")),
            P(None, "row"),
        ),
        out_specs=P("col", "freq", "row"),
        check_vma=False,
    )
```

```python
import functools

import jax
import jax.numpy as jnp
import ml_dtypes
import numpy as np
from jax import lax
from jax.experimental import pallas as pl
from jax.experimental.pallas import tpu as pltpu
from jax.sharding import PartitionSpec as P

NT = 1024
decay = 2.0
bin_step = 37

MESH = pl.DeviceIdType.MESH
BF16 = jnp.bfloat16
F32 = jnp.float32

NX, NZ = 4, 8
FREQS = 4
NFOC = 16
OWN = 3
PART = NZ * 64

Z_FIRST, X_FIRST = 0, 1
TILES = (5, 3)


def tile(f, d):
    if d == 0:
        return Z_FIRST, f
    return (Z_FIRST, 4) if f == 0 else (X_FIRST, f - 1)

def gather_kernel(
    refl, panels, out, rbuf, praw, held_z, held_x, pmat, acc, sendbuf, slots,
    load_sem, h_send, h_recv, e_send, e_recv,
):
    held = (held_z, held_x)
    freq = lax.axis_index("freq")
    row = lax.axis_index("row")
    col = lax.axis_index("col")
    x, z = row // NZ, row % NZ
    core, far = col % 2, col // 2

    along = {("z", d): {"row": x * NZ + (z + d + NZ) % NZ} for d in (1, -1, 2, -2)}
    along |= {("x", d): {"row": ((x + d + NX) % NX) * NZ + z} for d in (1, -1, 2)}

    def column(b):
        return (far + b // 2) % 2 * 2 + (core + b) % 2

    def peer(a, b):
        return {"freq": (freq + a) % 2, "col": column(b)}

    peers = ((0, 2), (0, 3), (1, 2), (1, 3), (1, 0), (1, 1), (0, 1))

    barrier = pltpu.get_barrier_semaphore()
    near = list(along.values()) + [peer(a, b) for a, b in peers]
    for device in near:
        pl.semaphore_signal(barrier, inc=1, device_id=device, device_id_type=MESH)

    load_panels = pltpu.make_async_copy(panels, praw, load_sem.at[FREQS])
    load_panels.start()
    loads = [pltpu.make_async_copy(refl.at[f], rbuf.at[f], load_sem.at[f]) for f in range(FREQS)]
    for load in loads:
        load.start()
    load_panels.wait()

    odd = (z % 2) == 1
    for f in range(FREQS):
        for d in range(2):
            re = praw[f, 0, d].astype(F32)
            im = praw[f, 1, d].astype(F32)
            left = jnp.where(odd, im, re)
            right = jnp.where(odd, re, im)
            kind, i = tile(f, d)
            held[kind][0, OWN, i] = jnp.concatenate([left, right], axis=1).astype(BF16)

    pl.semaphore_wait(barrier, len(near))

    started = []

    def start(copies):
        for copy in copies:
            copy.start()
            started.append(copy)

    def arrived(copies):
        for copy in copies:
            copy.wait_recv()

    def slot(dx, dz):
        return dx % NX, (4 if dz == -4 else dz) + OWN

    def hop(kind, dx, dz, axis, step, count=1):
        there = slot(dx + step, dz) if axis == "x" else slot(dx, dz + step)
        (x_from, z_from), (x_to, z_to) = slot(dx, dz), there
        return pltpu.make_async_remote_copy(
            src_ref=held[kind].at[x_from, pl.ds(z_from, count)],
            dst_ref=held[kind].at[x_to, pl.ds(z_to, count)],
            send_sem=h_send.at[kind, x_to, z_to],
            recv_sem=h_recv.at[kind, x_to, z_to],
            device_id=along[axis, step],
            device_id_type=MESH,
        )

    def here(kind, dx, dz, count=1):
        x_at, z_at = slot(dx, dz)
        at = held[kind].at[x_at, pl.ds(z_at, count)]
        return pltpu.make_async_remote_copy(
            src_ref=at,
            dst_ref=at,
            send_sem=h_send.at[kind, x_at, z_at],
            recv_sem=h_recv.at[kind, x_at, z_at],
            device_id=along["x", 1],
            device_id_type=MESH,
        )

    def round_x(kind, dz, count=1):
        return [hop(kind, 0, dz, "x", step, count) for step in (2, 1, -1)]

    def along_z(kind, dx, dz):
        if dz == 0:
            steps = (2, -2, 1, -1)
        else:
            way = dz // 2
            both = way == (1 if kind == Z_FIRST or dx == 0 else -1)
            steps = (2 * way, way) if both else (way,)
        return [hop(kind, dx, dz, "z", step) for step in steps]

    over_sources = (((1,), (1,)), ((), ()))
    lower = lax.broadcasted_iota(jnp.int32, (NFOC, 128), 1) < 64
    z_slots = [(z - za + OWN + NZ) % NZ for za in range(NZ)]

    def multiply(f, ways):
        found = [acc[f, m] if 0 not in ways else None for m in range(2)]
        for i, dx in enumerate(ways):
            for d in range(2):
                kind, t = tile(f, d)
                for zp in range(NZ // 2):
                    even = held[kind][dx % NX, z_slots[2 * zp], t].astype(F32)
                    uneven = held[kind][dx % NX, z_slots[2 * zp + 1], t].astype(F32)
                    re = jnp.where(lower, even, uneven)
                    im = pltpu.roll(jnp.where(lower, uneven, even), 64, 1)
                    at = pl.ds(i * PART + zp * 128, 128)
                    pmat[pl.ds(d * 16, 16), at] = re.astype(BF16)
                    pmat[pl.ds(32 + d * 16, 16), at] = im.astype(BF16)
        for i, dx in enumerate(ways):
            sources = pl.ds(pl.multiple_of((x - dx + NX) % NX * PART, PART), PART)
            for m in range(2):
                more = lax.dot_general(
                    pmat[:, i * PART : i * PART + PART],
                    rbuf[f, m, :, sources],
                    over_sources,
                    preferred_element_type=F32,
                )
                found[m] = more if found[m] is None else found[m] + more
        for m in range(2):
            acc[f, m] = found[m]

    def e_copy(f, a, b):
        return pltpu.make_async_remote_copy(
            src_ref=sendbuf.at[f, column(b)],
            dst_ref=slots.at[f, a, b],
            send_sem=e_send.at[f, a, b],
            recv_sem=e_recv.at[f, a, b],
            device_id=peer(a, b),
            device_id_type=MESH,
        )

    def combine(f):
        for q in range(4):
            here = pl.ds(8 * q, 8)
            there = pl.ds(32 + 8 * q, 8)
            if q < 2:
                sendbuf[f, q, 0] = acc[f, 0, here] - acc[f, 1, there]
                sendbuf[f, q, 1] = acc[f, 0, there] + acc[f, 1, here]
            else:
                sendbuf[f, q, 0] = acc[f, 0, here] + acc[f, 1, there]
                sendbuf[f, q, 1] = acc[f, 0, there] - acc[f, 1, here]
        start([e_copy(f, a, b) for a, b in peers])

    def keep(k, part, value):
        for h in range(out.shape[0]):
            out[h, pl.ds((k * 2 + part) * 8, 8), :] = value[:, 128 * h : 128 * h + 128]

    start(along_z(Z_FIRST, 0, 0))
    start(round_x(X_FIRST, 0))
    start(round_x(Z_FIRST, 0))
    start(along_z(X_FIRST, 0, 0))
    for dx in (1, -1):
        arrived([here(X_FIRST, dx, 0)])
        start(along_z(X_FIRST, dx, 0))
    for dz in (2, -2):
        arrived([here(Z_FIRST, 0, dz)])
        start(along_z(Z_FIRST, 0, dz))
    arrived([here(X_FIRST, 2, 0)])
    start(along_z(X_FIRST, 2, 0))
    for dz in (1, -1):
        arrived([here(Z_FIRST, 0, dz)])
    for dz in (1, -2):
        start(round_x(Z_FIRST, dz, 2))
    for dx in (0, 1, -1):
        for dz in (2, -2):
            arrived([here(X_FIRST, dx, dz)])
            start(along_z(X_FIRST, dx, dz))
    arrived([here(Z_FIRST, 0, dz) for dz in (3, 4)])
    start(round_x(Z_FIRST, 3, 2))
    arrived([here(Z_FIRST, 0, -3)])
    start(round_x(Z_FIRST, -3))
    for dz in (2, -2):
        arrived([here(X_FIRST, 2, dz)])
        start(along_z(X_FIRST, 2, dz))
    gathering, started[:] = list(started), []

    for f in range(FREQS):
        if f == 1:
            arrived([here(X_FIRST, 0, dz) for dz in (1, -1, 3, -3, 4)])
        loads[f].wait()
        multiply(f, (0,))
    for dx in (1, -1, 2):
        arrived([here(Z_FIRST, dx, 0)])
        arrived([here(Z_FIRST, dx, dz, 2) for dz in (1, -2, 3)])
        arrived([here(Z_FIRST, dx, -3)])
    for f in range(FREQS):
        if f == 1:
            for dx in (1, -1, 2):
                arrived([here(X_FIRST, dx, dz) for dz in (1, -1, 3, -3, 4)])
        multiply(f, (1, -1, 2))
        combine(f)
    for copy in gathering:
        copy.wait_send()
    for f in range(FREQS):
        arrived([e_copy(f, a, b) for a, b in peers])
        for part in range(2):
            own = sendbuf[f, col, part] + slots[f, 0, 1, part]
            keep(f, part, own + (slots[f, 0, 2, part] + slots[f, 0, 3, part]))
            other = slots[f, 1, 0, part] + slots[f, 1, 1, part]
            keep(f + FREQS, part, other + (slots[f, 1, 2, part] + slots[f, 1, 3, part]))
    for copy in started:
        copy.wait_send()


def times_kernel(spectra, table, onsets, out, series, out_sem):
    freq = lax.axis_index("freq")
    col = lax.axis_index("col")
    steps = series.shape[1]
    width = series.shape[2]
    basis = table[freq]
    times = freq * steps + lax.broadcasted_iota(jnp.int32, (steps, width), 0)
    limits = onsets[pl.ds(pl.multiple_of(col % 2 * 8, 8), 8), :]
    copies = []
    for c in range(8):
        values = jnp.concatenate(
            [spectra[h, pl.ds(c, 16, stride=8), :] for h in range(width // 128)], axis=1
        )
        high = values.astype(BF16)
        low = (values - high.astype(F32)).astype(BF16)
        parts = jnp.concatenate([high, high, low, low], axis=0)
        found = jnp.dot(basis, parts, preferred_element_type=F32)
        series[c] = jnp.where(times < limits[c : c + 1, :], found, 0.0)
        copy = pltpu.make_async_copy(series.at[c], out.at[c], out_sem.at[c])
        copy.start()
        copies.append(copy)
    for copy in copies:
        copy.wait()


def make_table(groups, freq_here):
    total = groups * freq_here
    t = np.arange(NT, dtype=np.int64)
    weight = np.exp(-decay * t / NT) / np.sqrt(total)
    halves = []
    for g in range(groups):
        mine = slice(g * NT // groups, (g + 1) * NT // groups)
        columns = []
        for a in range(groups):
            for f in range(freq_here):
                k = (g + a) % groups * freq_here + f
                phase = 2.0 * np.pi * ((bin_step * (k + 1) * t) % NT) / NT
                columns += [(np.cos(phase) * weight)[mine], (-np.sin(phase) * weight)[mine]]
        whole = np.stack(columns, axis=1)
        high = whole.astype(np.float32).astype(ml_dtypes.bfloat16)
        low = (whole - high.astype(np.float64)).astype(np.float32).astype(ml_dtypes.bfloat16)
        halves.append(np.concatenate([high, low, high, low], axis=1))
    return np.stack(halves)


def shards(reflection, panels, onsets):
    receivers = reflection.shape[2]
    vmem = pl.BlockSpec(memory_space=pltpu.VMEM)
    hbm = pl.BlockSpec(memory_space=pltpu.HBM)
    panels = pltpu.with_memory_space_constraint(panels, pltpu.HBM)
    spectra = pl.pallas_call(
        gather_kernel,
        out_shape=jax.ShapeDtypeStruct((receivers // 128, 128, 128), F32),
        in_specs=[hbm, hbm],
        out_specs=vmem,
        scratch_shapes=[
            pltpu.VMEM(reflection.shape, BF16),
            pltpu.VMEM(panels.shape, BF16),
            *[pltpu.VMEM((NX, NZ, count, NFOC, 128), BF16) for count in TILES],
            pltpu.VMEM((64, 3 * PART), BF16),
            pltpu.VMEM((FREQS, 2, 64, receivers), F32),
            pltpu.VMEM((FREQS, 4, 2, 8, receivers), F32),
            pltpu.VMEM((FREQS, 2, 4, 2, 8, receivers), F32),
            pltpu.SemaphoreType.DMA((FREQS + 1,)),
            pltpu.SemaphoreType.DMA((2, NX, NZ)),
            pltpu.SemaphoreType.DMA((2, NX, NZ)),
            pltpu.SemaphoreType.DMA((FREQS, 2, 4)),
            pltpu.SemaphoreType.DMA((FREQS, 2, 4)),
        ],
        compiler_params=pltpu.CompilerParams(collective_id=0, has_side_effects=True, vmem_limit_bytes=48 << 20),
        name="gather_products",
    )(reflection, panels)
    groups = lax.axis_size("freq")
    steps = NT // groups
    table = jnp.asarray(make_table(groups, reflection.shape[0]))
    return pl.pallas_call(
        times_kernel,
        out_shape=jax.ShapeDtypeStruct((8, steps, receivers), F32),
        in_specs=[vmem, vmem, vmem],
        out_specs=hbm,
        scratch_shapes=[pltpu.VMEM((8, steps, receivers), F32), pltpu.SemaphoreType.DMA((8,))],
        compiler_params=pltpu.CompilerParams(vmem_limit_bytes=48 << 20),
        name="to_times",
    )(spectra, table, onsets)


def solution(mesh):
    return jax.shard_map(
        shards,
        mesh=mesh,
        in_specs=(
            P("freq", None, "row", "col"),
            P("freq", None, None, None, ("col", "row")),
            P(None, "row"),
        ),
        out_specs=P("col", "freq", "row"),
        check_vma=False,
    )
```

```python
import functools

import jax
import jax.numpy as jnp
import ml_dtypes
import numpy as np
from jax import lax
from jax.experimental import pallas as pl
from jax.experimental.pallas import tpu as pltpu
from jax.sharding import PartitionSpec as P

NT = 1024
decay = 2.0
bin_step = 37

MESH = pl.DeviceIdType.MESH
BF16 = jnp.bfloat16
F32 = jnp.float32

NX, NZ = 4, 8
FREQS = 4
NFOC = 16
OWN = 3
PART = NZ * 64

Z_FIRST, X_FIRST = 0, 1
TILES = (5, 3)


def tile(f, d):
    if d == 0:
        return Z_FIRST, f
    return (Z_FIRST, 4) if f == 0 else (X_FIRST, f - 1)

def gather_kernel(
    refl, panels, out, rbuf, praw, held_z, held_x, pmat, acc, sendbuf, slots,
    load_sem, h_send, h_recv, e_send, e_recv,
):
    held = (held_z, held_x)
    freq = lax.axis_index("freq")
    row = lax.axis_index("row")
    col = lax.axis_index("col")
    x, z = row // NZ, row % NZ
    core, far = col % 2, col // 2

    along = {("z", d): {"row": x * NZ + (z + d + NZ) % NZ} for d in (1, -1, 2, -2)}
    along |= {("x", d): {"row": ((x + d + NX) % NX) * NZ + z} for d in (1, -1, 2)}

    def column(b):
        return (far + b // 2) % 2 * 2 + (core + b) % 2

    def peer(a, b):
        return {"freq": (freq + a) % 2, "col": column(b)}

    peers = ((0, 2), (0, 3), (1, 2), (1, 3), (1, 0), (1, 1), (0, 1))

    load_panels = pltpu.make_async_copy(panels, praw, load_sem.at[FREQS])
    load_panels.start()
    barrier = pltpu.get_barrier_semaphore()
    near = list(along.values()) + [peer(a, b) for a, b in peers]
    for device in near:
        pl.semaphore_signal(barrier, inc=1, device_id=device, device_id_type=MESH)

    loads = [pltpu.make_async_copy(refl.at[f], rbuf.at[f], load_sem.at[f]) for f in range(FREQS)]
    load_panels.wait()

    odd = (z % 2) == 1
    for f in range(FREQS):
        for d in range(2):
            re = praw[f, 0, d].astype(F32)
            im = praw[f, 1, d].astype(F32)
            left = jnp.where(odd, im, re)
            right = jnp.where(odd, re, im)
            kind, i = tile(f, d)
            held[kind][0, OWN, i] = jnp.concatenate([left, right], axis=1).astype(BF16)

    pl.semaphore_wait(barrier, len(near))

    started = []

    def start(copies):
        for copy in copies:
            copy.start()
            started.append(copy)

    def arrived(copies):
        for copy in copies:
            copy.wait_recv()

    def slot(dx, dz):
        return dx % NX, (4 if dz == -4 else dz) + OWN

    def hop(kind, dx, dz, axis, step, count=1):
        there = slot(dx + step, dz) if axis == "x" else slot(dx, dz + step)
        (x_from, z_from), (x_to, z_to) = slot(dx, dz), there
        return pltpu.make_async_remote_copy(
            src_ref=held[kind].at[x_from, pl.ds(z_from, count)],
            dst_ref=held[kind].at[x_to, pl.ds(z_to, count)],
            send_sem=h_send.at[kind, x_to, z_to],
            recv_sem=h_recv.at[kind, x_to, z_to],
            device_id=along[axis, step],
            device_id_type=MESH,
        )

    def here(kind, dx, dz, count=1):
        x_at, z_at = slot(dx, dz)
        at = held[kind].at[x_at, pl.ds(z_at, count)]
        return pltpu.make_async_remote_copy(
            src_ref=at,
            dst_ref=at,
            send_sem=h_send.at[kind, x_at, z_at],
            recv_sem=h_recv.at[kind, x_at, z_at],
            device_id=along["x", 1],
            device_id_type=MESH,
        )

    def round_x(kind, dz, count=1):
        return [hop(kind, 0, dz, "x", step, count) for step in (2, 1, -1)]

    def along_z(kind, dx, dz):
        if dz == 0:
            steps = (2, -2, 1, -1)
        else:
            way = dz // 2
            both = way == (1 if kind == Z_FIRST or dx == 0 else -1)
            steps = (2 * way, way) if both else (way,)
        return [hop(kind, dx, dz, "z", step) for step in steps]

    over_sources = (((1,), (1,)), ((), ()))
    lower = lax.broadcasted_iota(jnp.int32, (NFOC, 128), 1) < 64
    z_slots = [(z - za + OWN + NZ) % NZ for za in range(NZ)]

    def multiply(f, ways):
        found = [acc[f, m] if 0 not in ways else None for m in range(2)]
        for i, dx in enumerate(ways):
            for d in range(2):
                kind, t = tile(f, d)
                for zp in range(NZ // 2):
                    even = held[kind][dx % NX, z_slots[2 * zp], t].astype(F32)
                    uneven = held[kind][dx % NX, z_slots[2 * zp + 1], t].astype(F32)
                    re = jnp.where(lower, even, uneven)
                    im = pltpu.roll(jnp.where(lower, uneven, even), 64, 1)
                    at = pl.ds(i * PART + zp * 128, 128)
                    pmat[pl.ds(d * 16, 16), at] = re.astype(BF16)
                    pmat[pl.ds(32 + d * 16, 16), at] = im.astype(BF16)
        for i, dx in enumerate(ways):
            sources = pl.ds(pl.multiple_of((x - dx + NX) % NX * PART, PART), PART)
            for m in range(2):
                more = lax.dot_general(
                    pmat[:, i * PART : i * PART + PART],
                    rbuf[f, m, :, sources],
                    over_sources,
                    preferred_element_type=F32,
                )
                found[m] = more if found[m] is None else found[m] + more
        for m in range(2):
            acc[f, m] = found[m]

    def e_copy(f, a, b):
        return pltpu.make_async_remote_copy(
            src_ref=sendbuf.at[f, column(b)],
            dst_ref=slots.at[f, a, b],
            send_sem=e_send.at[f, a, b],
            recv_sem=e_recv.at[f, a, b],
            device_id=peer(a, b),
            device_id_type=MESH,
        )

    def combine(f):
        for q in range(4):
            here = pl.ds(8 * q, 8)
            there = pl.ds(32 + 8 * q, 8)
            if q < 2:
                sendbuf[f, q, 0] = acc[f, 0, here] - acc[f, 1, there]
                sendbuf[f, q, 1] = acc[f, 0, there] + acc[f, 1, here]
            else:
                sendbuf[f, q, 0] = acc[f, 0, here] + acc[f, 1, there]
                sendbuf[f, q, 1] = acc[f, 0, there] - acc[f, 1, here]
        start([e_copy(f, a, b) for a, b in peers])

    def keep(k, part, value):
        for h in range(out.shape[0]):
            out[h, pl.ds((k * 2 + part) * 8, 8), :] = value[:, 128 * h : 128 * h + 128]

    start(along_z(Z_FIRST, 0, 0))
    start(round_x(X_FIRST, 0))
    start(round_x(Z_FIRST, 0))
    start(along_z(X_FIRST, 0, 0))
    for load in loads:
        load.start()
    for dx in (1, -1):
        arrived([here(X_FIRST, dx, 0)])
        start(along_z(X_FIRST, dx, 0))
    for dz in (2, -2):
        arrived([here(Z_FIRST, 0, dz)])
        start(along_z(Z_FIRST, 0, dz))
    arrived([here(X_FIRST, 2, 0)])
    start(along_z(X_FIRST, 2, 0))
    for dz in (1, -1):
        arrived([here(Z_FIRST, 0, dz)])
    for dz in (1, -2):
        start(round_x(Z_FIRST, dz, 2))
    for dx in (0, 1, -1):
        for dz in (2, -2):
            arrived([here(X_FIRST, dx, dz)])
            start(along_z(X_FIRST, dx, dz))
    for dz in (3, -3, 4):
        arrived([here(Z_FIRST, 0, dz)])
        start(round_x(Z_FIRST, dz))
    for dz in (2, -2):
        arrived([here(X_FIRST, 2, dz)])
        start(along_z(X_FIRST, 2, dz))
    gathering, started[:] = list(started), []

    for f in range(FREQS):
        if f == 1:
            arrived([here(X_FIRST, 0, dz) for dz in (1, -1, 3, -3, 4)])
        loads[f].wait()
        multiply(f, (0,))
    for dx in (1, -1, 2):
        arrived([here(Z_FIRST, dx, 0)])
        arrived([here(Z_FIRST, dx, dz, 2) for dz in (1, -2)])
        arrived([here(Z_FIRST, dx, dz) for dz in (3, -3, 4)])
    for f in range(FREQS):
        if f == 1:
            for dx in (1, -1, 2):
                arrived([here(X_FIRST, dx, dz) for dz in (1, -1, 3, -3, 4)])
        multiply(f, (1, -1, 2))
        combine(f)
    for copy in gathering + started:
        copy.wait_send()
    for f in range(FREQS):
        arrived([e_copy(f, a, b) for a, b in peers])
        for part in range(2):
            own = sendbuf[f, col, part] + slots[f, 0, 1, part]
            keep(f, part, own + (slots[f, 0, 2, part] + slots[f, 0, 3, part]))
            other = slots[f, 1, 0, part] + slots[f, 1, 1, part]
            keep(f + FREQS, part, other + (slots[f, 1, 2, part] + slots[f, 1, 3, part]))


def times_kernel(spectra, table, onsets, out, series, out_sem):
    freq = lax.axis_index("freq")
    col = lax.axis_index("col")
    steps = series.shape[1]
    width = series.shape[2]
    basis = table[freq]
    times = freq * steps + lax.broadcasted_iota(jnp.int32, (steps, width), 0)
    limits = onsets[pl.ds(pl.multiple_of(col % 2 * 8, 8), 8), :]
    copies = []
    for c in range(8):
        values = jnp.concatenate(
            [spectra[h, pl.ds(c, 16, stride=8), :] for h in range(width // 128)], axis=1
        )
        high = values.astype(BF16)
        low = (values - high.astype(F32)).astype(BF16)
        parts = jnp.concatenate([high, high, low, low], axis=0)
        found = jnp.dot(basis, parts, preferred_element_type=F32)
        series[c] = jnp.where(times < limits[c : c + 1, :], found, 0.0)
        copy = pltpu.make_async_copy(series.at[c], out.at[c], out_sem.at[c])
        copy.start()
        copies.append(copy)
    for copy in copies:
        copy.wait()


def make_table(groups, freq_here):
    total = groups * freq_here
    t = np.arange(NT, dtype=np.int64)
    weight = np.exp(-decay * t / NT) / np.sqrt(total)
    halves = []
    for g in range(groups):
        mine = slice(g * NT // groups, (g + 1) * NT // groups)
        columns = []
        for a in range(groups):
            for f in range(freq_here):
                k = (g + a) % groups * freq_here + f
                phase = 2.0 * np.pi * ((bin_step * (k + 1) * t) % NT) / NT
                columns += [(np.cos(phase) * weight)[mine], (-np.sin(phase) * weight)[mine]]
        whole = np.stack(columns, axis=1)
        high = whole.astype(np.float32).astype(ml_dtypes.bfloat16)
        low = (whole - high.astype(np.float64)).astype(np.float32).astype(ml_dtypes.bfloat16)
        halves.append(np.concatenate([high, low, high, low], axis=1))
    return np.stack(halves)


def shards(reflection, panels, onsets):
    receivers = reflection.shape[2]
    vmem = pl.BlockSpec(memory_space=pltpu.VMEM)
    hbm = pl.BlockSpec(memory_space=pltpu.HBM)
    panels = pltpu.with_memory_space_constraint(panels, pltpu.HBM)
    spectra = pl.pallas_call(
        gather_kernel,
        out_shape=jax.ShapeDtypeStruct((receivers // 128, 128, 128), F32),
        in_specs=[hbm, hbm],
        out_specs=vmem,
        scratch_shapes=[
            pltpu.VMEM(reflection.shape, BF16),
            pltpu.VMEM(panels.shape, BF16),
            *[pltpu.VMEM((NX, NZ, count, NFOC, 128), BF16) for count in TILES],
            pltpu.VMEM((64, 3 * PART), BF16),
            pltpu.VMEM((FREQS, 2, 64, receivers), F32),
            pltpu.VMEM((FREQS, 4, 2, 8, receivers), F32),
            pltpu.VMEM((FREQS, 2, 4, 2, 8, receivers), F32),
            pltpu.SemaphoreType.DMA((FREQS + 1,)),
            pltpu.SemaphoreType.DMA((2, NX, NZ)),
            pltpu.SemaphoreType.DMA((2, NX, NZ)),
            pltpu.SemaphoreType.DMA((FREQS, 2, 4)),
            pltpu.SemaphoreType.DMA((FREQS, 2, 4)),
        ],
        compiler_params=pltpu.CompilerParams(collective_id=0, has_side_effects=True, vmem_limit_bytes=48 << 20),
        name="gather_products",
    )(reflection, panels)
    groups = lax.axis_size("freq")
    steps = NT // groups
    table = jnp.asarray(make_table(groups, reflection.shape[0]))
    return pl.pallas_call(
        times_kernel,
        out_shape=jax.ShapeDtypeStruct((8, steps, receivers), F32),
        in_specs=[vmem, vmem, vmem],
        out_specs=hbm,
        scratch_shapes=[pltpu.VMEM((8, steps, receivers), F32), pltpu.SemaphoreType.DMA((8,))],
        compiler_params=pltpu.CompilerParams(vmem_limit_bytes=48 << 20),
        name="to_times",
    )(spectra, table, onsets)


def solution(mesh):
    return jax.shard_map(
        shards,
        mesh=mesh,
        in_specs=(
            P("freq", None, "row", "col"),
            P("freq", None, None, None, ("col", "row")),
            P(None, "row"),
        ),
        out_specs=P("col", "freq", "row"),
        check_vma=False,
    )
```
